32 devices in a mesh: grp: 2 (over y), row: 4 (over z), col: 2 (over x), sub: 2 (over core).
Axes of the slice: x: 2, y: 2, z: 4, core: 2. Of those that a mesh axis runs over, the one named last changes fastest.
Arguments:
- fine_field: bfloat16 [64, 512, 1024], P(('grp', 'row'), None, ('col', 'sub')), parts along dimension 0, may hold values from -6 to 6
- conv_taps: bfloat16 [3, 3, 1024], P(None, None, ('col', 'sub')), may hold values from -1 to 1
- position_table: bfloat16 [256, 1024], P(None, ('col', 'sub')), may hold values from -3 to 3
- coarse_bands: bfloat16 [8, 34, 64], P(('grp', 'row')), parts along dimension 0, may hold values from -6 to 6
- band_weight: bfloat16 [34, 2048], replicated, may hold values from -3 to 3
- noise_step: int32 [1], replicated, may hold values from 0 to 17
- land_tiles: int32 [64, 4], P(('grp', 'row')), parts along dimension 0, may hold values from 0 to 1, as said below
- tile_owner: int32 [64, 4], P(('grp', 'row')), parts along dimension 0, may hold values from 0 to 3, as said below
- neighbour_lists: int32 [64, 4, 128], P(('grp', 'row')), parts along dimension 0, may hold values from 0 to 511
- tile_order: int32 [64, 4, 128], P(('grp', 'row')), parts along dimension 0, may hold values from 0 to 127, each once within a row
- expert_projections: bfloat16 [4, 1024, 3, 1024], P('row', None, None, ('col', 'sub'))
- expert_output: bfloat16 [4, 1024, 1024], P('row', ('col', 'sub')), may hold values from -0.1875 to 0.1875
Outputs:
- denoised: bfloat16 [64, 512, 1024], P(('grp', 'row'), None, ('col', 'sub')), parts along dimension 0
The draws below stay inside these ranges and needn't reach their ends.
There are 2 independent parts, one for each index of `grp`. The reference program is written for one: setup_inputs(seed, part) draws one part's arguments, and reference() takes and returns one part's arrays. A program takes and returns all parts, laid end to end along the dimension named above; an argument that names none is the same for every part. Nothing has to cross between parts.
Inputs may be any that keep to these rules, and one draw needn't show every extreme that they name: `land_tiles`: every strip (the 8 latitude rows that one index of row holds) has 8 or more land tiles. `tile_owner`: of the land tiles of one strip at most 8 have the same owner; in every draw some owner has exactly 8 land tiles of every strip.
All inputs are finite; a program needn't handle non-finite values.
Results may differ from the reference program's by a relative error of at most 0.0087.
Values may be sent and summed in bfloat16 or wider, within the bound.
A program may use at most 128 MiB of HBM per device.

```python
import math
import jax
import jax.numpy as jnp
from jax import lax

D = 1024
HEAD = 64
CC = 34
TILE = 128
COARSE = 8
DIFF_STEPS = 18
NLON = 512
NLAT = 32
TPR = 4
SLOTS = 32
EXPERTS = 4
BANDS = 4
NLON_C = 64


def tile_layout(key):
    base_key = jax.random.fold_in(key, 11)
    key_count, key_order, key_busy, key_rank = jax.random.split(base_key, 4)
    per_owner = SLOTS // EXPERTS
    counts = jax.random.randint(key_count, (EXPERTS, 1), per_owner, SLOTS + 1)
    tile_rank = jax.vmap(lambda row_key: jax.random.permutation(row_key, SLOTS))(jax.random.split(key_order, EXPERTS)).astype(jnp.int32)
    busy_owner = jax.random.randint(key_busy, (), 0, EXPERTS)
    slot_rank = jax.vmap(lambda row_key: jax.random.permutation(row_key, SLOTS))(jax.random.split(key_rank, EXPERTS)).astype(jnp.int32)
    slot_ids = jnp.arange(SLOTS, dtype=jnp.int32)[None, :]
    priority = jnp.where(slot_ids // per_owner == busy_owner, slot_ids - SLOTS, slot_rank)
    slot_order = jnp.argsort(priority, axis=1, stable=True).astype(jnp.int32)
    position = jnp.arange(SLOTS, dtype=jnp.int32)[None, :]
    is_land = (position < counts).astype(jnp.int32)
    owner_of = (slot_order // per_owner).astype(jnp.int32)
    strips = jnp.arange(EXPERTS, dtype=jnp.int32)[:, None]
    land_map = jnp.zeros((EXPERTS, SLOTS), jnp.int32).at[strips, tile_rank].set(is_land)
    owner_map = jnp.zeros((EXPERTS, SLOTS), jnp.int32).at[strips, tile_rank].set(owner_of)
    return (land_map.reshape(NLAT, NLON // TILE), owner_map.reshape(NLAT, NLON // TILE))


def draw_land_tiles(key, part):
    return tile_layout(key)[0]


def draw_tile_owner(key, part):
    return tile_layout(key)[1]


def draw_expert_projections(key, part):
    base_key = jax.random.fold_in(key, 23)
    key_main = jax.random.fold_in(base_key, 0)
    spread = 1.5 / math.sqrt(D)
    weights = jax.random.normal(key_main, (EXPERTS, D, 3, D), jnp.float32) * spread
    return weights.astype(jnp.bfloat16)


def plant(drawn, rng, smallest, top_value):
    dims = drawn.shape
    index_at = [jax.random.randint(jax.random.fold_in(rng, axis), (), 0, dims[axis]) for axis in range(len(dims))]
    drawn = drawn.at[tuple(index_at)].set(smallest)
    longest = dims.index(max(dims))
    index_at[longest] = (index_at[longest] + 1) % dims[longest]
    return drawn.at[tuple(index_at)].set(top_value)


def shard_levels(key, dims, cuts, low, largest):
    level = 1.0
    for axis_at, blocks in cuts:
        draws = jax.random.uniform(jax.random.fold_in(jax.random.fold_in(key, 6), axis_at), (blocks,), jnp.float32, low / len(cuts), largest / len(cuts))
        level = level * jnp.repeat(jnp.exp(draws), dims[axis_at] // blocks).reshape((-1,) + (1,) * (len(dims) - 1 - axis_at))
    return level


def bell_draw(stream_key, shape, scale, most, shards=(), held_as=jnp.bfloat16):
    entries = jax.random.normal(stream_key, shape, jnp.float32) * scale
    if len(shards) > 0:
        entries = shard_levels(stream_key, shape, shards, -0.22, 0.18) * entries
    return jnp.clip(entries, min=-most, max=most).astype(held_as)


def setup_inputs(seed: int = 0, part: int = 0) -> dict:
    key_of = jax.random.split(jax.random.key(seed), 13)
    own_keys = jax.random.split(jax.random.fold_in(key_of[12], part), 13)
    fine_field = bell_draw(own_keys[0], (NLAT, NLON, D), 1.0, 6.0, ((0, 4), (2, 4)))
    conv_taps = bell_draw(key_of[1], (3, 3, D), 0.25, 1.0, ((2, 4),))
    position_table = bell_draw(key_of[2], (2 * TILE, D), 0.5, 3.0, ((1, 4),))
    coarse_bands = bell_draw(own_keys[3], (BANDS, CC, NLON_C), 1.0, 6.0, ((0, 4),))
    band_weight = bell_draw(key_of[4], (CC, 2 * D), 0.5, 3.0)
    noise_step = jax.random.randint(key_of[5], (1,), 0, DIFF_STEPS).astype(jnp.int32)
    land_tiles = draw_land_tiles(jax.random.fold_in(jax.random.fold_in(key_of[12], part), 71), part)
    tile_owner = draw_tile_owner(jax.random.fold_in(jax.random.fold_in(key_of[12], part), 71), part)
    neighbour_lists = plant(jax.random.randint(own_keys[8], (NLAT, TPR, TILE), 0, NLON), jax.random.fold_in(own_keys[8], 1), 0, NLON - 1).astype(jnp.int32)
    tile_order = jax.vmap(lambda own: jax.random.permutation(own, TILE))(jax.random.split(own_keys[9], NLAT * TPR)).reshape((NLAT, TPR, TILE)).astype(jnp.int32)
    expert_projections = draw_expert_projections(jax.random.fold_in(key_of[12], 71), part)
    expert_output = bell_draw(key_of[11], (EXPERTS, D, D), D ** -0.5, 0.1875, ((0, 4), (1, 4)))
    return dict(fine_field=fine_field, conv_taps=conv_taps, position_table=position_table, coarse_bands=coarse_bands, band_weight=band_weight, noise_step=noise_step, land_tiles=land_tiles, tile_owner=tile_owner, neighbour_lists=neighbour_lists, tile_order=tile_order, expert_projections=expert_projections, expert_output=expert_output)


EPSILON = 1e-05

def step_embedding(noise_step, emb_width):
    positions = jnp.arange(emb_width, dtype=jnp.float32)
    frequency = jnp.exp(-4.0 * positions / emb_width)
    return 0.5 * jnp.sin((noise_step[0].astype(jnp.float32) + 1.0) * frequency)

def attend_block(inputs, scale_rows, shift_rows, projection, out_weight):
    values = inputs.astype(jnp.float32)
    average = lax.optimization_barrier(jnp.mean(values, axis=-1, keepdims=True))
    centred = values - average
    variance = lax.optimization_barrier(jnp.mean(centred * centred, axis=-1, keepdims=True))
    normed = centred * lax.rsqrt(variance + EPSILON)
    hidden = (normed * (1.0 + scale_rows[:, None, :]) + shift_rows[:, None, :]).astype(jnp.bfloat16)
    slot_count = inputs.shape[0]
    widths = projection.shape[2]
    head_count = widths // HEAD
    hidden_wide = hidden.astype(jnp.float32)
    queries = jnp.einsum('sqd,dw->sqw', hidden_wide[:, :TILE], projection[:, 0].astype(jnp.float32)).astype(jnp.bfloat16)
    key_values = jnp.einsum('skd,dtw->sktw', hidden_wide, projection[:, 1:].astype(jnp.float32)).astype(jnp.bfloat16)
    query_heads = queries.astype(jnp.float32).reshape(slot_count, TILE, head_count, HEAD)
    key_heads = key_values[:, :, 0].astype(jnp.float32).reshape(slot_count, -1, head_count, HEAD)
    value_heads = key_values[:, :, 1].astype(jnp.float32).reshape(slot_count, -1, head_count, HEAD)
    scores = jnp.einsum('sqhe,skhe->shqk', query_heads, key_heads) * (1.0 / math.sqrt(HEAD))
    highest = lax.optimization_barrier(jnp.max(scores, axis=-1, keepdims=True))
    weights = jnp.exp(scores - highest)
    chances = (weights / lax.optimization_barrier(jnp.sum(weights, axis=-1, keepdims=True))).astype(jnp.bfloat16)
    mixture = jnp.einsum('shqk,skhe->sqhe', chances.astype(jnp.float32), value_heads).astype(jnp.bfloat16)
    mixture = mixture.reshape(slot_count, TILE, widths)
    return jnp.einsum('sqw,wd->sqd', mixture.astype(jnp.float32), out_weight.astype(jnp.float32))

def reference(fine_field, conv_taps, position_table, coarse_bands, band_weight, noise_step, land_tiles, tile_owner, neighbour_lists, tile_order, expert_projections, expert_output):
    padded = jnp.pad(fine_field, ((1, 1), (1, 1), (0, 0)))
    tap_values = conv_taps.astype(jnp.float32)

    def convolve_row(lat_index):
        window = lax.dynamic_slice_in_dim(padded, lat_index, 3, 0).astype(jnp.float32)
        running = lax.dynamic_index_in_dim(fine_field, lat_index, 0, keepdims=False).astype(jnp.float32)
        for row_shift in range(3):
            for col_shift in range(3):
                running = running + tap_values[row_shift, col_shift] * window[row_shift, col_shift:col_shift + NLON]
        return running.astype(jnp.bfloat16)
    smoothed = lax.map(convolve_row, jnp.arange(NLAT, dtype=jnp.int32))
    band_means = lax.optimization_barrier(jnp.mean(coarse_bands.astype(jnp.float32), axis=2))
    modulation = jnp.dot(band_means, band_weight.astype(jnp.float32), precision=lax.Precision.HIGHEST) + step_embedding(noise_step, band_weight.shape[1])

    def one_tile(tile_id):
        lat_index = tile_id // TPR
        tile_col = tile_id % TPR
        lat_row = lax.dynamic_index_in_dim(smoothed, lat_index, 0, keepdims=False)
        tile_cells = lax.dynamic_slice_in_dim(lat_row, tile_col * TILE, TILE, 0)
        within = tile_order[lat_index, tile_col]
        neighbours = neighbour_lists[lat_index, tile_col]
        sequence = jnp.concatenate([tile_cells[within], lat_row[neighbours]], axis=0)
        inputs = (sequence.astype(jnp.float32) + position_table.astype(jnp.float32)).astype(jnp.bfloat16)
        band_row = lax.dynamic_index_in_dim(modulation, lat_index // COARSE, 0, keepdims=True)
        expert = tile_owner[lat_index, tile_col]

        def on_land(operand):
            result = attend_block(inputs[None], band_row[:, :D], band_row[:, D:], expert_projections[expert], expert_output[expert])[0].astype(jnp.bfloat16)
            placed = jnp.zeros((TILE, D), jnp.float32).at[within].set(result.astype(jnp.float32))
            return (tile_cells.astype(jnp.float32) + placed).astype(jnp.bfloat16)

        def at_sea(operand):
            return tile_cells
        return lax.cond(land_tiles[lat_index, tile_col] > 0, on_land, at_sea, 0)
    tile_results = lax.map(one_tile, jnp.arange(NLAT * TPR, dtype=jnp.int32))
    return tile_results.reshape(NLAT, NLON, D)
```

```python
import functools
import math

import jax
import jax.numpy as jnp
from jax import lax
from jax.experimental import pallas as pl
from jax.experimental.pallas import tpu as pltpu
from jax.sharding import PartitionSpec as P

HEAD = 64
TILE = 128


EPSILON = 1e-05


def extended(cells, sides, width):
    for axis, dim in sides:
        count = lax.axis_size(axis)
        ends = count - 1
        head = lax.slice_in_dim(cells, 0, width, axis=dim)
        tail = lax.slice_in_dim(cells, cells.shape[dim] - width, cells.shape[dim], axis=dim)
        cells = jnp.concatenate(
            [
                lax.ppermute(tail, axis, [(i, (i + 1) % count) for i in range(ends)]),
                cells,
                lax.ppermute(head, axis, [((i + 1) % count, i) for i in range(ends)]),
            ],
            axis=dim,
        )
    return cells


def step_embedding(noise_step, emb_width):
    positions = jnp.arange(emb_width, dtype=jnp.float32)
    frequency = jnp.exp(-4.0 * positions / emb_width)
    return 0.5 * jnp.sin((noise_step[0].astype(jnp.float32) + 1.0) * frequency)


def gather_kernel(tile_ref, field_ref, index_ref, table_ref, out_ref):
    tile = tile_ref[pl.program_id(0)]
    table = index_ref[...]
    lanes = lax.broadcasted_iota(jnp.int32, table.shape, 1)
    column = jnp.sum(jnp.where(lanes == tile, table, 0), axis=1, keepdims=True)
    cells = field_ref.shape[1]
    spots = lax.broadcasted_iota(jnp.int32, (table.shape[0], cells), 1)
    select = jnp.where(spots == column, 1.0, 0.0).astype(jnp.bfloat16)
    picked = jnp.dot(select, field_ref[0], preferred_element_type=jnp.float32)
    out_ref[0] = (picked + table_ref[...].astype(jnp.float32)).astype(jnp.bfloat16)


def gather_tiles(smoothed, tile_of, index_table, position_table, tiles_row):
    lat_rows, lon_cells, channels = smoothed.shape
    tokens, tile_count = index_table.shape
    return pl.pallas_call(
        gather_kernel,
        grid_spec=pltpu.PrefetchScalarGridSpec(
            num_scalar_prefetch=1,
            grid=(tile_count,),
            in_specs=[
                pl.BlockSpec((1, lon_cells, channels), lambda s, t: (t[s] // tiles_row, 0, 0)),
                pl.BlockSpec((tokens, tile_count), lambda s, t: (0, 0)),
                pl.BlockSpec((tokens, channels), lambda s, t: (0, 0)),
            ],
            out_specs=pl.BlockSpec((1, tokens, channels), lambda s, t: (s, 0, 0)),
        ),
        out_shape=jax.ShapeDtypeStruct((tile_count, tokens, channels), jnp.bfloat16),
        compiler_params=pltpu.CompilerParams(vmem_limit_bytes=32 * 1024 * 1024),
        cost_estimate=pl.CostEstimate(
            flops=2 * tile_count * tokens * lon_cells * channels,
            bytes_accessed=2 * tile_count * (lon_cells + tokens) * channels,
            transcendentals=0,
        ),
        name="gather_tiles",
    )(tile_of, smoothed, index_table, position_table)


def merge_kernel(tiles_row, slot_ref, land_ref, field_ref, order_ref, *refs):
    out_ref = refs[-1]
    row = pl.program_id(0)
    for col in range(tiles_row):
        span = pl.ds(col * TILE, TILE)
        spots = lax.broadcasted_iota(jnp.int32, (TILE, TILE), 0)
        place = jnp.where(spots == order_ref[0, col : col + 1, :], 1.0, 0.0).astype(jnp.bfloat16)
        moved = jnp.dot(place, refs[col][0], preferred_element_type=jnp.float32)
        kept = field_ref[0, span, :]
        added = (kept.astype(jnp.float32) + moved).astype(jnp.bfloat16)
        is_land = land_ref[row * tiles_row + col] > 0
        out_ref[0, span, :] = jnp.where(is_land, added, kept)


def merge_tiles(smoothed, results, slot_of, land, tile_order):
    lat_rows, lon_cells, channels = smoothed.shape
    tiles_row = tile_order.shape[1]

    def picked(col):
        return pl.BlockSpec(
            (1, TILE, channels), lambda r, s, m: (s[r * tiles_row + col], 0, 0)
        )

    return pl.pallas_call(
        functools.partial(merge_kernel, tiles_row),
        grid_spec=pltpu.PrefetchScalarGridSpec(
            num_scalar_prefetch=2,
            grid=(lat_rows,),
            in_specs=[
                pl.BlockSpec((1, lon_cells, channels), lambda r, s, m: (r, 0, 0)),
                pl.BlockSpec((1, tiles_row, TILE), lambda r, s, m: (r, 0, 0)),
            ]
            + [picked(col) for col in range(tiles_row)],
            out_specs=pl.BlockSpec((1, lon_cells, channels), lambda r, s, m: (r, 0, 0)),
        ),
        out_shape=jax.ShapeDtypeStruct(smoothed.shape, jnp.bfloat16),
        compiler_params=pltpu.CompilerParams(vmem_limit_bytes=32 * 1024 * 1024),
        name="merge_tiles",
    )(slot_of, land, smoothed, tile_order, *([results] * tiles_row))


def attend_kernel(x_ref, scale_ref, shift_ref, proj_ref, weight_ref, out_ref):
    parts = x_ref.shape[0]
    width = x_ref.shape[3]
    heads = width // HEAD
    tokens = x_ref.shape[2]
    full = parts * width
    values = [x_ref[g, 0].astype(jnp.float32) for g in range(parts)]
    average = sum(jnp.sum(v, axis=-1, keepdims=True) for v in values) * (1.0 / full)
    centred = [v - average for v in values]
    variance = sum(jnp.sum(v * v, axis=-1, keepdims=True) for v in centred) * (1.0 / full)
    inverse = lax.rsqrt(variance + EPSILON)
    hidden = jnp.concatenate(
        [
            (
                v * inverse * (1.0 + scale_ref[0, :, g * width : (g + 1) * width])
                + shift_ref[0, :, g * width : (g + 1) * width]
            ).astype(jnp.bfloat16)
            for g, v in enumerate(centred)
        ],
        axis=1,
    )
    lane_head = lax.broadcasted_iota(jnp.int32, (TILE, width), 1) // HEAD
    total = jnp.zeros((TILE, full), jnp.float32)
    for g in range(parts):
        queries = jnp.dot(hidden[:TILE], proj_ref[g, 0], preferred_element_type=jnp.float32)
        queries = queries * (1.0 / math.sqrt(HEAD))
        keys = jnp.dot(hidden, proj_ref[g, 1], preferred_element_type=jnp.float32).astype(jnp.bfloat16)
        vals = jnp.dot(hidden, proj_ref[g, 2], preferred_element_type=jnp.float32).astype(jnp.bfloat16)
        stacked = jnp.concatenate(
            [jnp.where(lane_head == h, queries, 0.0).astype(jnp.bfloat16) for h in range(heads)], axis=0
        )
        scores = lax.dot_general(
            stacked, keys, (((1,), (1,)), ((), ())), preferred_element_type=jnp.float32
        )
        weights = jnp.exp(scores - jnp.max(scores, axis=-1, keepdims=True))
        chances = (weights * (1.0 / jnp.sum(weights, axis=-1, keepdims=True))).astype(jnp.bfloat16)
        mixed = jnp.dot(chances, vals, preferred_element_type=jnp.float32)
        mixture = mixed[:TILE]
        for h in range(1, heads):
            mixture = jnp.where(lane_head == h, mixed[h * TILE : (h + 1) * TILE], mixture)
        total = total + jnp.dot(
            mixture.astype(jnp.bfloat16), weight_ref[g], preferred_element_type=jnp.float32
        )
    for g in range(parts):
        out_ref[g, 0] = total[:, g * width : (g + 1) * width].astype(jnp.bfloat16)


def attend(inputs, scale, shift, projection, out_weight):
    parts, slots, tokens, width = inputs.shape
    full = parts * width
    whole = lambda s: (0, 0, 0, 0)
    return pl.pallas_call(
        attend_kernel,
        grid=(slots,),
        in_specs=[
            pl.BlockSpec((parts, 1, tokens, width), lambda s: (0, s, 0, 0)),
            pl.BlockSpec((1, 1, full), lambda s: (s, 0, 0)),
            pl.BlockSpec((1, 1, full), lambda s: (s, 0, 0)),
            pl.BlockSpec(projection.shape, whole),
            pl.BlockSpec(out_weight.shape, lambda s: (0, 0, 0)),
        ],
        out_specs=pl.BlockSpec((parts, 1, TILE, width), lambda s: (0, s, 0, 0)),
        out_shape=jax.ShapeDtypeStruct((parts, slots, TILE, width), jnp.bfloat16),
        compiler_params=pltpu.CompilerParams(vmem_limit_bytes=48 * 1024 * 1024),
        cost_estimate=pl.CostEstimate(
            flops=slots * 2 * tokens * full * full * 4,
            bytes_accessed=2 * (slots * 2 * tokens * full + 4 * full * full),
            transcendentals=slots * tokens * tokens * 8,
        ),
        name="attend",
    )(inputs, scale[:, None, :], shift[:, None, :], projection, out_weight)


def pick_rows(mod_table, first_slot, slot_total, per_source):
    sources = (first_slot + jnp.arange(slot_total, dtype=jnp.int32)) // per_source
    select = (sources[:, None] == jnp.arange(mod_table.shape[0], dtype=jnp.int32)[None, :]).astype(
        jnp.float32
    )
    return jnp.dot(select, mod_table, precision=lax.Precision.HIGHEST)


def body(
    fine_field,
    conv_taps,
    position_table,
    coarse_bands,
    band_weight,
    noise_step,
    land_tiles,
    tile_owner,
    neighbour_lists,
    tile_order,
    expert_projections,
    expert_output,
):
    lat_rows, lon_cells, channels = fine_field.shape
    tiles_row = land_tiles.shape[1]
    tile_count = lat_rows * tiles_row
    strips = lax.axis_size("row")
    per_owner = tile_count // strips
    padded = extended(fine_field, (("row", 0),), 1)
    padded = jnp.pad(padded, ((0, 0), (1, 1), (0, 0)))
    tap_values = conv_taps.astype(jnp.float32)
    running = fine_field.astype(jnp.float32)
    for row_shift in range(3):
        for col_shift in range(3):
            running = running + tap_values[row_shift, col_shift] * padded[
                row_shift : row_shift + lat_rows, col_shift : col_shift + lon_cells
            ].astype(jnp.float32)
    smoothed = running.astype(jnp.bfloat16)
    land_flat = land_tiles.reshape(tile_count)
    owner_flat = tile_owner.reshape(tile_count)
    tile_ids = jnp.arange(tile_count, dtype=jnp.int32)
    earlier = (
        (owner_flat[None, :] == owner_flat[:, None])
        & (land_flat[None, :] > 0)
        & (tile_ids[None, :] < tile_ids[:, None])
    )
    slot_rank = jnp.sum(earlier.astype(jnp.int32), axis=1)
    slot_of = owner_flat * per_owner + slot_rank
    chosen = ((slot_of[None, :] == tile_ids[:, None]) & (land_flat[None, :] > 0)).astype(jnp.int32)
    tile_of = jnp.sum(chosen * tile_ids[None, :], axis=1)
    starts = (tile_ids % tiles_row) * TILE
    index_table = jnp.concatenate(
        [
            tile_order.reshape(tile_count, TILE) + starts[:, None],
            neighbour_lists.reshape(tile_count, TILE),
        ],
        axis=1,
    ).T
    sequence = gather_tiles(smoothed, tile_of, index_table, position_table, tiles_row)
    outgoing = sequence.reshape(strips, per_owner, 2 * TILE, channels)
    group_size = lax.axis_size(("col", "sub"))
    my_slots = tile_count // group_size
    arrived = lax.all_to_all(outgoing, "row", split_axis=0, concat_axis=0, tiled=True)
    arrived = arrived.reshape(group_size, my_slots, 2 * TILE, channels)
    gathered_bands = lax.all_gather(coarse_bands, "row", axis=0, tiled=True)
    band_means = jnp.mean(gathered_bands.astype(jnp.float32), axis=2)
    modulation = jnp.dot(
        band_means, band_weight.astype(jnp.float32), precision=lax.Precision.HIGHEST
    ) + step_embedding(noise_step, band_weight.shape[1])
    full_width = band_weight.shape[1] // 2
    inputs = lax.all_to_all(arrived, ("col", "sub"), split_axis=0, concat_axis=0, tiled=True)
    full_proj = lax.all_gather(
        jnp.transpose(expert_projections[0], (1, 0, 2)), ("col", "sub"), axis=0, tiled=False
    )
    full_out = lax.all_gather(expert_output[0], ("col", "sub"), axis=0, tiled=False)
    local_mod = pick_rows(
        modulation, lax.axis_index(("col", "sub")) * my_slots, my_slots, per_owner
    )
    heads_out = attend(
        inputs, local_mod[:, :full_width], local_mod[:, full_width:], full_proj, full_out
    )
    returned = lax.all_to_all(heads_out, ("col", "sub"), split_axis=0, concat_axis=0, tiled=True)
    returned = returned.reshape(strips, per_owner, TILE, channels)
    results = lax.all_to_all(returned, "row", split_axis=0, concat_axis=0, tiled=True)
    results = results.reshape(tile_count, TILE, channels)
    return merge_tiles(
        smoothed, results, jnp.minimum(slot_of, tile_count - 1), land_flat, tile_order
    )


def solution(mesh):
    placed = (
        P(("grp", "row"), None, ("col", "sub")),
        P(None, None, ("col", "sub")),
        P(None, ("col", "sub")),
        P(("grp", "row"), None, None),
        P(),
        P(),
        P(("grp", "row"), None),
        P(("grp", "row"), None),
        P(("grp", "row"), None, None),
        P(("grp", "row"), None, None),
        P("row", None, None, ("col", "sub")),
        P("row", ("col", "sub"), None),
    )
    return jax.shard_map(
        body,
        mesh=mesh,
        in_specs=placed,
        out_specs=P(("grp", "row"), None, ("col", "sub")),
        check_vma=False,
    )
```

```python
import functools
import math

import jax
import jax.numpy as jnp
from jax import lax
from jax.experimental import pallas as pl
from jax.experimental.pallas import tpu as pltpu
from jax.sharding import PartitionSpec as P

HEAD = 64
TILE = 128


EPSILON = 1e-05


def extended(cells, sides, width):
    for axis, dim in sides:
        count = lax.axis_size(axis)
        ends = count - 1
        head = lax.slice_in_dim(cells, 0, width, axis=dim)
        tail = lax.slice_in_dim(cells, cells.shape[dim] - width, cells.shape[dim], axis=dim)
        cells = jnp.concatenate(
            [
                lax.ppermute(tail, axis, [(i, (i + 1) % count) for i in range(ends)]),
                cells,
                lax.ppermute(head, axis, [((i + 1) % count, i) for i in range(ends)]),
            ],
            axis=dim,
        )
    return cells


def step_embedding(noise_step, emb_width):
    positions = jnp.arange(emb_width, dtype=jnp.float32)
    frequency = jnp.exp(-4.0 * positions / emb_width)
    return 0.5 * jnp.sin((noise_step[0].astype(jnp.float32) + 1.0) * frequency)


def gather_kernel(tile_ref, field_ref, index_ref, table_ref, out_ref):
    tile = tile_ref[pl.program_id(0)]
    table = index_ref[...]
    lanes = lax.broadcasted_iota(jnp.int32, table.shape, 1)
    column = jnp.sum(jnp.where(lanes == tile, table, 0), axis=1, keepdims=True)
    cells = field_ref.shape[1]
    spots = lax.broadcasted_iota(jnp.int32, (table.shape[0], cells), 1)
    select = jnp.where(spots == column, 1.0, 0.0).astype(jnp.bfloat16)
    picked = jnp.dot(select, field_ref[0], preferred_element_type=jnp.float32)
    out_ref[0] = (picked + table_ref[...].astype(jnp.float32)).astype(jnp.bfloat16)


def gather_tiles(smoothed, tile_of, index_table, position_table, tiles_row):
    lat_rows, lon_cells, channels = smoothed.shape
    tokens, tile_count = index_table.shape
    return pl.pallas_call(
        gather_kernel,
        grid_spec=pltpu.PrefetchScalarGridSpec(
            num_scalar_prefetch=1,
            grid=(tile_count,),
            in_specs=[
                pl.BlockSpec((1, lon_cells, channels), lambda s, t: (t[s] // tiles_row, 0, 0)),
                pl.BlockSpec((tokens, tile_count), lambda s, t: (0, 0)),
                pl.BlockSpec((tokens, channels), lambda s, t: (0, 0)),
            ],
            out_specs=pl.BlockSpec((1, tokens, channels), lambda s, t: (s, 0, 0)),
        ),
        out_shape=jax.ShapeDtypeStruct((tile_count, tokens, channels), jnp.bfloat16),
        compiler_params=pltpu.CompilerParams(vmem_limit_bytes=32 * 1024 * 1024),
        cost_estimate=pl.CostEstimate(
            flops=2 * tile_count * tokens * lon_cells * channels,
            bytes_accessed=2 * tile_count * (lon_cells + tokens) * channels,
            transcendentals=0,
        ),
        name="gather_tiles",
    )(tile_of, smoothed, index_table, position_table)


def merge_kernel(tiles_row, slot_ref, land_ref, field_ref, order_ref, *refs):
    out_ref = refs[-1]
    row = pl.program_id(0)
    for col in range(tiles_row):
        span = pl.ds(col * TILE, TILE)
        spots = lax.broadcasted_iota(jnp.int32, (TILE, TILE), 0)
        place = jnp.where(spots == order_ref[0, col : col + 1, :], 1.0, 0.0).astype(jnp.bfloat16)
        moved = jnp.dot(place, refs[col][0], preferred_element_type=jnp.float32)
        kept = field_ref[0, span, :]
        added = (kept.astype(jnp.float32) + moved).astype(jnp.bfloat16)
        is_land = land_ref[row * tiles_row + col] > 0
        out_ref[0, span, :] = jnp.where(is_land, added, kept)


def merge_tiles(smoothed, results, slot_of, land, tile_order):
    lat_rows, lon_cells, channels = smoothed.shape
    tiles_row = tile_order.shape[1]

    def picked(col):
        return pl.BlockSpec(
            (1, TILE, channels), lambda r, s, m: (s[r * tiles_row + col], 0, 0)
        )

    return pl.pallas_call(
        functools.partial(merge_kernel, tiles_row),
        grid_spec=pltpu.PrefetchScalarGridSpec(
            num_scalar_prefetch=2,
            grid=(lat_rows,),
            in_specs=[
                pl.BlockSpec((1, lon_cells, channels), lambda r, s, m: (r, 0, 0)),
                pl.BlockSpec((1, tiles_row, TILE), lambda r, s, m: (r, 0, 0)),
            ]
            + [picked(col) for col in range(tiles_row)],
            out_specs=pl.BlockSpec((1, lon_cells, channels), lambda r, s, m: (r, 0, 0)),
        ),
        out_shape=jax.ShapeDtypeStruct(smoothed.shape, jnp.bfloat16),
        compiler_params=pltpu.CompilerParams(vmem_limit_bytes=32 * 1024 * 1024),
        name="merge_tiles",
    )(slot_of, land, smoothed, tile_order, *([results] * tiles_row))


def attend_kernel(x_ref, scale_ref, shift_ref, proj_ref, weight_ref, out_ref):
    parts = x_ref.shape[0]
    width = x_ref.shape[3]
    heads = width // HEAD
    tokens = x_ref.shape[2]
    full = parts * width
    values = [x_ref[g, 0].astype(jnp.float32) for g in range(parts)]
    average = sum(jnp.sum(v, axis=-1, keepdims=True) for v in values) * (1.0 / full)
    centred = [v - average for v in values]
    variance = sum(jnp.sum(v * v, axis=-1, keepdims=True) for v in centred) * (1.0 / full)
    inverse = lax.rsqrt(variance + EPSILON)
    hidden = jnp.concatenate(
        [
            (
                v * inverse * (1.0 + scale_ref[0, :, g * width : (g + 1) * width])
                + shift_ref[0, :, g * width : (g + 1) * width]
            ).astype(jnp.bfloat16)
            for g, v in enumerate(centred)
        ],
        axis=1,
    )
    lane_head = lax.broadcasted_iota(jnp.int32, (TILE, width), 1) // HEAD
    total = jnp.zeros((TILE, full), jnp.float32)
    for g in range(parts):
        queries = jnp.dot(hidden[:TILE], proj_ref[g, 0], preferred_element_type=jnp.float32)
        queries = queries * (1.0 / math.sqrt(HEAD))
        keys = jnp.dot(hidden, proj_ref[g, 1], preferred_element_type=jnp.float32).astype(jnp.bfloat16)
        vals = jnp.dot(hidden, proj_ref[g, 2], preferred_element_type=jnp.float32).astype(jnp.bfloat16)
        stacked = jnp.concatenate(
            [jnp.where(lane_head == h, queries, 0.0).astype(jnp.bfloat16) for h in range(heads)], axis=0
        )
        scores = lax.dot_general(
            stacked, keys, (((1,), (1,)), ((), ())), preferred_element_type=jnp.float32
        )
        weights = jnp.exp(scores - jnp.max(scores, axis=-1, keepdims=True))
        chances = (weights * (1.0 / jnp.sum(weights, axis=-1, keepdims=True))).astype(jnp.bfloat16)
        mixed = jnp.dot(chances, vals, preferred_element_type=jnp.float32)
        mixture = mixed[:TILE]
        for h in range(1, heads):
            mixture = jnp.where(lane_head == h, mixed[h * TILE : (h + 1) * TILE], mixture)
        total = total + jnp.dot(
            mixture.astype(jnp.bfloat16), weight_ref[g], preferred_element_type=jnp.float32
        )
    for g in range(parts):
        out_ref[g, 0] = total[:, g * width : (g + 1) * width].astype(jnp.bfloat16)


def attend(inputs, scale, shift, projection, out_weight):
    parts, slots, tokens, width = inputs.shape
    full = parts * width
    whole = lambda s: (0, 0, 0, 0)
    return pl.pallas_call(
        attend_kernel,
        grid=(slots,),
        in_specs=[
            pl.BlockSpec((parts, 1, tokens, width), lambda s: (0, s, 0, 0)),
            pl.BlockSpec((1, 1, full), lambda s: (s, 0, 0)),
            pl.BlockSpec((1, 1, full), lambda s: (s, 0, 0)),
            pl.BlockSpec(projection.shape, whole),
            pl.BlockSpec(out_weight.shape, lambda s: (0, 0, 0)),
        ],
        out_specs=pl.BlockSpec((parts, 1, TILE, width), lambda s: (0, s, 0, 0)),
        out_shape=jax.ShapeDtypeStruct((parts, slots, TILE, width), jnp.bfloat16),
        compiler_params=pltpu.CompilerParams(vmem_limit_bytes=48 * 1024 * 1024),
        cost_estimate=pl.CostEstimate(
            flops=slots * 2 * tokens * full * full * 4,
            bytes_accessed=2 * (slots * 2 * tokens * full + 4 * full * full),
            transcendentals=slots * tokens * tokens * 8,
        ),
        name="attend",
    )(inputs, scale[:, None, :], shift[:, None, :], projection, out_weight)


def exchange_kernel(strips, group, forward, src_ref, dst_ref, send_sems, recv_sems, local_sem):
    row = lax.axis_index("row")
    subs = lax.axis_size("sub")
    mine = lax.axis_index("col") * subs + lax.axis_index("sub")
    share = (dst_ref if forward else src_ref).shape[1] // strips

    def target(step):
        there = lax.rem(row + step // group, strips)
        member = lax.rem(mine + step % group, group)
        return there, member

    def ends(there, member):
        if forward:
            source = src_ref.at[there, pl.ds(member * share, share)]
            return source, dst_ref.at[mine, pl.ds(row * share, share)]
        source = src_ref.at[member, pl.ds(there * share, share)]
        return source, dst_ref.at[row, pl.ds(mine * share, share)]

    def device(there, member):
        return {"row": there, "col": member // subs, "sub": lax.rem(member, subs)}

    def remote(step):
        there, member = target(step)
        source, dest = ends(there, member)
        return pltpu.make_async_remote_copy(
            src_ref=source,
            dst_ref=dest,
            send_sem=send_sems.at[step],
            recv_sem=recv_sems.at[step],
            device_id=device(there, member),
            device_id_type=pl.DeviceIdType.MESH,
        )

    total = strips * group
    barrier = pltpu.get_barrier_semaphore()
    source, dest = ends(row, mine)
    local = pltpu.make_async_copy(source, dest, local_sem)
    local.start()

    @pl.loop(1, total)
    def _(step):
        there, member = target(step)
        pl.semaphore_signal(
            barrier, inc=1, device_id=device(there, member), device_id_type=pl.DeviceIdType.MESH
        )

    pl.semaphore_wait(barrier, total - 1)

    @pl.loop(1, total)
    def _(step):
        remote(total - step).start()

    local.wait()

    @pl.loop(1, total)
    def _(step):
        remote(step).wait()


def exchange(array, strips, group, forward):
    first, second, tokens, width = array.shape
    if forward:
        shape = (group, strips * (second // group), tokens, width)
    else:
        shape = (strips, group * (second // strips), tokens, width)
    total = strips * group
    return pl.pallas_call(
        functools.partial(exchange_kernel, strips, group, forward),
        out_shape=jax.ShapeDtypeStruct(shape, array.dtype),
        in_specs=[pl.BlockSpec(memory_space=pl.ANY)],
        out_specs=pl.BlockSpec(memory_space=pl.ANY),
        scratch_shapes=[
            pltpu.SemaphoreType.DMA((total,)),
            pltpu.SemaphoreType.DMA((total,)),
            pltpu.SemaphoreType.DMA,
        ],
        compiler_params=pltpu.CompilerParams(
            collective_id=0 if forward else 1, has_side_effects=True
        ),
        cost_estimate=pl.CostEstimate(
            flops=0, bytes_accessed=(64 if forward else 32) * array.size, transcendentals=0
        ),
        name="send_tiles" if forward else "return_tiles",
    )(array)


def pick_rows(mod_table, first_slot, slot_total, per_source):
    sources = (first_slot + jnp.arange(slot_total, dtype=jnp.int32)) // per_source
    select = (sources[:, None] == jnp.arange(mod_table.shape[0], dtype=jnp.int32)[None, :]).astype(
        jnp.float32
    )
    return jnp.dot(select, mod_table, precision=lax.Precision.HIGHEST)


def body(
    fine_field,
    conv_taps,
    position_table,
    coarse_bands,
    band_weight,
    noise_step,
    land_tiles,
    tile_owner,
    neighbour_lists,
    tile_order,
    expert_projections,
    expert_output,
):
    lat_rows, lon_cells, channels = fine_field.shape
    tiles_row = land_tiles.shape[1]
    tile_count = lat_rows * tiles_row
    strips = lax.axis_size("row")
    per_owner = tile_count // strips
    padded = extended(fine_field, (("row", 0),), 1)
    padded = jnp.pad(padded, ((0, 0), (1, 1), (0, 0)))
    tap_values = conv_taps.astype(jnp.float32)
    running = fine_field.astype(jnp.float32)
    for row_shift in range(3):
        for col_shift in range(3):
            running = running + tap_values[row_shift, col_shift] * padded[
                row_shift : row_shift + lat_rows, col_shift : col_shift + lon_cells
            ].astype(jnp.float32)
    smoothed = running.astype(jnp.bfloat16)
    land_flat = land_tiles.reshape(tile_count)
    owner_flat = tile_owner.reshape(tile_count)
    tile_ids = jnp.arange(tile_count, dtype=jnp.int32)
    earlier = (
        (owner_flat[None, :] == owner_flat[:, None])
        & (land_flat[None, :] > 0)
        & (tile_ids[None, :] < tile_ids[:, None])
    )
    slot_rank = jnp.sum(earlier.astype(jnp.int32), axis=1)
    slot_of = owner_flat * per_owner + slot_rank
    chosen = ((slot_of[None, :] == tile_ids[:, None]) & (land_flat[None, :] > 0)).astype(jnp.int32)
    tile_of = jnp.sum(chosen * tile_ids[None, :], axis=1)
    starts = (tile_ids % tiles_row) * TILE
    index_table = jnp.concatenate(
        [
            tile_order.reshape(tile_count, TILE) + starts[:, None],
            neighbour_lists.reshape(tile_count, TILE),
        ],
        axis=1,
    ).T
    sequence = gather_tiles(smoothed, tile_of, index_table, position_table, tiles_row)
    outgoing = sequence.reshape(strips, per_owner, 2 * TILE, channels)
    group_size = lax.axis_size(("col", "sub"))
    my_slots = tile_count // group_size
    direct = per_owner % group_size == 0
    gathered_bands = lax.all_gather(coarse_bands, "row", axis=0, tiled=True)
    band_means = jnp.mean(gathered_bands.astype(jnp.float32), axis=2)
    modulation = jnp.dot(
        band_means, band_weight.astype(jnp.float32), precision=lax.Precision.HIGHEST
    ) + step_embedding(noise_step, band_weight.shape[1])
    full_width = band_weight.shape[1] // 2
    if direct:
        inputs = exchange(outgoing, strips, group_size, True)
    else:
        arrived = lax.all_to_all(outgoing, "row", split_axis=0, concat_axis=0, tiled=True)
        arrived = arrived.reshape(group_size, my_slots, 2 * TILE, channels)
        inputs = lax.all_to_all(arrived, ("col", "sub"), split_axis=0, concat_axis=0, tiled=True)
    full_proj = lax.all_gather(
        jnp.transpose(expert_projections[0], (1, 0, 2)), ("col", "sub"), axis=0, tiled=False
    )
    full_out = lax.all_gather(expert_output[0], ("col", "sub"), axis=0, tiled=False)
    if direct:
        local_mod = pick_rows(modulation, 0, my_slots, per_owner // group_size)
    else:
        local_mod = pick_rows(
            modulation, lax.axis_index(("col", "sub")) * my_slots, my_slots, per_owner
        )
    heads_out = attend(
        inputs, local_mod[:, :full_width], local_mod[:, full_width:], full_proj, full_out
    )
    if direct:
        results = exchange(heads_out, strips, group_size, False)
    else:
        returned = lax.all_to_all(heads_out, ("col", "sub"), split_axis=0, concat_axis=0, tiled=True)
        returned = returned.reshape(strips, per_owner, TILE, channels)
        results = lax.all_to_all(returned, "row", split_axis=0, concat_axis=0, tiled=True)
    results = results.reshape(tile_count, TILE, channels)
    return merge_tiles(
        smoothed, results, jnp.minimum(slot_of, tile_count - 1), land_flat, tile_order
    )


def solution(mesh):
    placed = (
        P(("grp", "row"), None, ("col", "sub")),
        P(None, None, ("col", "sub")),
        P(None, ("col", "sub")),
        P(("grp", "row"), None, None),
        P(),
        P(),
        P(("grp", "row"), None),
        P(("grp", "row"), None),
        P(("grp", "row"), None, None),
        P(("grp", "row"), None, None),
        P("row", None, None, ("col", "sub")),
        P("row", ("col", "sub"), None),
    )
    return jax.shard_map(
        body,
        mesh=mesh,
        in_specs=placed,
        out_specs=P(("grp", "row"), None, ("col", "sub")),
        check_vma=False,
    )
```

```python
import functools
import math

import jax
import jax.numpy as jnp
from jax import lax
from jax.experimental import pallas as pl
from jax.experimental.pallas import tpu as pltpu
from jax.sharding import PartitionSpec as P

HEAD = 64
TILE = 128


EPSILON = 1e-05


def extended(cells, sides, width):
    for axis, dim in sides:
        count = lax.axis_size(axis)
        ends = count - 1
        head = lax.slice_in_dim(cells, 0, width, axis=dim)
        tail = lax.slice_in_dim(cells, cells.shape[dim] - width, cells.shape[dim], axis=dim)
        cells = jnp.concatenate(
            [
                lax.ppermute(tail, axis, [(i, (i + 1) % count) for i in range(ends)]),
                cells,
                lax.ppermute(head, axis, [((i + 1) % count, i) for i in range(ends)]),
            ],
            axis=dim,
        )
    return cells


def step_embedding(noise_step, emb_width):
    positions = jnp.arange(emb_width, dtype=jnp.float32)
    frequency = jnp.exp(-4.0 * positions / emb_width)
    return 0.5 * jnp.sin((noise_step[0].astype(jnp.float32) + 1.0) * frequency)


def gather_kernel(tile_ref, field_ref, index_ref, table_ref, out_ref):
    tile = tile_ref[pl.program_id(0)]
    table = index_ref[...]
    lanes = lax.broadcasted_iota(jnp.int32, table.shape, 1)
    column = jnp.sum(jnp.where(lanes == tile, table, 0), axis=1, keepdims=True)
    cells = field_ref.shape[1]
    spots = lax.broadcasted_iota(jnp.int32, (table.shape[0], cells), 1)
    select = jnp.where(spots == column, 1.0, 0.0).astype(jnp.bfloat16)
    picked = jnp.dot(select, field_ref[0], preferred_element_type=jnp.float32)
    out_ref[0] = (picked + table_ref[...].astype(jnp.float32)).astype(jnp.bfloat16)


def gather_tiles(smoothed, tile_of, index_table, position_table, tiles_row):
    lat_rows, lon_cells, channels = smoothed.shape
    tokens, tile_count = index_table.shape
    return pl.pallas_call(
        gather_kernel,
        grid_spec=pltpu.PrefetchScalarGridSpec(
            num_scalar_prefetch=1,
            grid=(tile_count,),
            in_specs=[
                pl.BlockSpec((1, lon_cells, channels), lambda s, t: (t[s] // tiles_row, 0, 0)),
                pl.BlockSpec((tokens, tile_count), lambda s, t: (0, 0)),
                pl.BlockSpec((tokens, channels), lambda s, t: (0, 0)),
            ],
            out_specs=pl.BlockSpec((1, tokens, channels), lambda s, t: (s, 0, 0)),
        ),
        out_shape=jax.ShapeDtypeStruct((tile_count, tokens, channels), jnp.bfloat16),
        compiler_params=pltpu.CompilerParams(vmem_limit_bytes=32 * 1024 * 1024),
        cost_estimate=pl.CostEstimate(
            flops=2 * tile_count * tokens * lon_cells * channels,
            bytes_accessed=2 * tile_count * (lon_cells + tokens) * channels,
            transcendentals=0,
        ),
        name="gather_tiles",
    )(tile_of, smoothed, index_table, position_table)


def merge_kernel(tiles_row, slot_ref, land_ref, field_ref, order_ref, *refs):
    out_ref = refs[-1]
    row = pl.program_id(0)
    for col in range(tiles_row):
        span = pl.ds(col * TILE, TILE)
        spots = lax.broadcasted_iota(jnp.int32, (TILE, TILE), 0)
        place = jnp.where(spots == order_ref[0, col : col + 1, :], 1.0, 0.0).astype(jnp.bfloat16)
        moved = jnp.dot(place, refs[col][0], preferred_element_type=jnp.float32)
        kept = field_ref[0, span, :]
        added = (kept.astype(jnp.float32) + moved).astype(jnp.bfloat16)
        is_land = land_ref[row * tiles_row + col] > 0
        out_ref[0, span, :] = jnp.where(is_land, added, kept)


def merge_tiles(smoothed, results, slot_of, land, tile_order):
    lat_rows, lon_cells, channels = smoothed.shape
    tiles_row = tile_order.shape[1]

    def picked(col):
        return pl.BlockSpec(
            (1, TILE, channels), lambda r, s, m: (s[r * tiles_row + col], 0, 0)
        )

    return pl.pallas_call(
        functools.partial(merge_kernel, tiles_row),
        grid_spec=pltpu.PrefetchScalarGridSpec(
            num_scalar_prefetch=2,
            grid=(lat_rows,),
            in_specs=[
                pl.BlockSpec((1, lon_cells, channels), lambda r, s, m: (r, 0, 0)),
                pl.BlockSpec((1, tiles_row, TILE), lambda r, s, m: (r, 0, 0)),
            ]
            + [picked(col) for col in range(tiles_row)],
            out_specs=pl.BlockSpec((1, lon_cells, channels), lambda r, s, m: (r, 0, 0)),
        ),
        out_shape=jax.ShapeDtypeStruct(smoothed.shape, jnp.bfloat16),
        compiler_params=pltpu.CompilerParams(vmem_limit_bytes=32 * 1024 * 1024),
        name="merge_tiles",
    )(slot_of, land, smoothed, tile_order, *([results] * tiles_row))


def attend_slot(values, scale, shift, proj_ref, weight_ref):
    parts, width = len(values), values[0].shape[1]
    heads = width // HEAD
    full = parts * width
    average = sum(jnp.sum(v, axis=-1, keepdims=True) for v in values) * (1.0 / full)
    centred = [v - average for v in values]
    variance = sum(jnp.sum(v * v, axis=-1, keepdims=True) for v in centred) * (1.0 / full)
    inverse = lax.rsqrt(variance + EPSILON)
    hidden = jnp.concatenate(
        [
            (
                v * inverse * (1.0 + scale[:, g * width : (g + 1) * width])
                + shift[:, g * width : (g + 1) * width]
            ).astype(jnp.bfloat16)
            for g, v in enumerate(centred)
        ],
        axis=1,
    )
    lane_head = lax.broadcasted_iota(jnp.int32, (TILE, width), 1) // HEAD
    total = jnp.zeros((TILE, full), jnp.float32)
    for g in range(parts):
        queries = jnp.dot(hidden[:TILE], proj_ref[g, 0], preferred_element_type=jnp.float32)
        queries = queries * (1.0 / math.sqrt(HEAD))
        keys = jnp.dot(hidden, proj_ref[g, 1], preferred_element_type=jnp.float32).astype(jnp.bfloat16)
        vals = jnp.dot(hidden, proj_ref[g, 2], preferred_element_type=jnp.float32).astype(jnp.bfloat16)
        stacked = jnp.concatenate(
            [jnp.where(lane_head == h, queries, 0.0).astype(jnp.bfloat16) for h in range(heads)], axis=0
        )
        scores = lax.dot_general(
            stacked, keys, (((1,), (1,)), ((), ())), preferred_element_type=jnp.float32
        )
        weights = jnp.exp(scores - jnp.max(scores, axis=-1, keepdims=True))
        chances = (weights * (1.0 / jnp.sum(weights, axis=-1, keepdims=True))).astype(jnp.bfloat16)
        mixed = jnp.dot(chances, vals, preferred_element_type=jnp.float32)
        mixture = mixed[:TILE]
        for h in range(1, heads):
            mixture = jnp.where(lane_head == h, mixed[h * TILE : (h + 1) * TILE], mixture)
        total = total + jnp.dot(
            mixture.astype(jnp.bfloat16), weight_ref[g], preferred_element_type=jnp.float32
        )
    return [total[:, g * width : (g + 1) * width].astype(jnp.bfloat16) for g in range(parts)]


def attend_kernel(x_ref, scale_ref, shift_ref, proj_ref, weight_ref, out_ref):
    values = [x_ref[g, 0].astype(jnp.float32) for g in range(x_ref.shape[0])]
    pieces = attend_slot(values, scale_ref[0], shift_ref[0], proj_ref, weight_ref)
    for g, piece in enumerate(pieces):
        out_ref[g, 0] = piece


def travel_kernel(
    strips,
    cols,
    subs,
    seq_ref,
    mod_ref,
    own_proj_ref,
    own_weight_ref,
    out_ref,
    tokens,
    mods,
    proj,
    weight,
    done,
    seq_send,
    seq_recv,
    back_send,
    back_recv,
    mod_send,
    mod_recv,
    far_send,
    far_recv,
    near_send,
    near_recv,
    local_sems,
):
    group = cols * subs
    total = strips * group
    row = lax.axis_index("row")
    col = lax.axis_index("col")
    sub = lax.axis_index("sub")
    mine = col * subs + sub
    slots = tokens.shape[1]
    share = slots // strips
    full = mods.shape[2] // 2

    def device(there, member):
        return {"row": there, "col": member // subs, "sub": lax.rem(member, subs)}

    def remote(source, dest, send, recv, there, member):
        return pltpu.make_async_remote_copy(
            src_ref=source,
            dst_ref=dest,
            send_sem=send,
            recv_sem=recv,
            device_id=device(there, member),
            device_id_type=pl.DeviceIdType.MESH,
        )

    def seq_ends(there, member):
        return (
            seq_ref.at[there, pl.ds(member * share, share)],
            tokens.at[mine, pl.ds(row * share, share)],
        )

    def seq_copy(step):
        there, member = lax.rem(row + step // group, strips), lax.rem(mine + step % group, group)
        source, dest = seq_ends(there, member)
        return remote(source, dest, seq_send.at[step], seq_recv.at[step], there, member)

    def back_ends(there, member):
        return (
            done.at[member, pl.ds(there * share, share)],
            out_ref.at[row, pl.ds(mine * share, share)],
        )

    def back_copy(step):
        there = lax.rem(row + strips - step // group, strips)
        member = lax.rem(mine + step % group, group)
        source, dest = back_ends(there, member)
        return remote(source, dest, back_send.at[step], back_recv.at[step], there, member)

    def mod_copy(step):
        there = lax.rem(row + step, strips)
        return remote(mod_ref, mods.at[row], mod_send.at[step], mod_recv.at[step], there, mine)

    pairs = ((own_proj_ref, proj), (own_weight_ref, weight))

    def far_copy(step, kind):
        source, held = pairs[kind]
        member = lax.rem(col + step, cols) * subs + sub
        at = step * 2 + kind
        return remote(source, held.at[mine], far_send.at[at], far_recv.at[at], row, member)

    def near_copy(step, hop, kind):
        source, held = pairs[kind]
        owner = lax.rem(col + cols - step, cols) * subs + sub
        member = col * subs + lax.rem(sub + hop, subs)
        at = (step * subs + hop) * 2 + kind
        return remote(
            source if step == 0 else held.at[owner],
            held.at[owner],
            near_send.at[at],
            near_recv.at[at],
            row,
            member,
        )

    seq_local = pltpu.make_async_copy(*seq_ends(row, mine), local_sems.at[0])
    back_local = pltpu.make_async_copy(*back_ends(row, mine), local_sems.at[1])
    locals_ = [
        pltpu.make_async_copy(mod_ref, mods.at[row], local_sems.at[2]),
        pltpu.make_async_copy(own_proj_ref, proj.at[mine], local_sems.at[3]),
        pltpu.make_async_copy(own_weight_ref, weight.at[mine], local_sems.at[4]),
    ]
    seq_local.start()
    for copy in locals_:
        copy.start()

    barrier = pltpu.get_barrier_semaphore()

    @pl.loop(1, total)
    def _(step):
        there, member = lax.rem(row + step // group, strips), lax.rem(mine + step % group, group)
        pl.semaphore_signal(
            barrier, inc=1, device_id=device(there, member), device_id_type=pl.DeviceIdType.MESH
        )

    pl.semaphore_wait(barrier, total - 1)

    for kind in range(2):
        for step in range(1, cols):
            far_copy(step, kind).start()
        for hop in range(1, subs):
            near_copy(0, hop, kind).start()
    for step in range(1, strips):
        mod_copy(step).start()

    @pl.loop(1, total)
    def _(step):
        seq_copy(step).start()

    for kind in range(2):
        for step in range(1, cols):
            far_copy(step, kind).wait_recv()
            for hop in range(1, subs):
                near_copy(step, hop, kind).start()
    for copy in locals_:
        copy.wait()
    for step in range(1, strips):
        mod_copy(step).wait_recv()
    for kind in range(2):
        for step in range(cols):
            for hop in range(1, subs):
                near_copy(step, hop, kind).wait_recv()
    seq_local.wait()

    @pl.loop(0, strips)
    def _(turn):
        there = lax.rem(row + strips - turn, strips)

        @pl.loop(0, group)
        def _(member):
            @pl.when(turn * group + member > 0)
            def _():
                seq_copy(turn * group + member).wait_recv()

        @pl.loop(0, share)
        def _(index):
            slot = there * share + index
            values = [tokens[g, slot].astype(jnp.float32) for g in range(group)]
            rows = mods[there]
            pieces = attend_slot(values, rows[0:1, :full], rows[0:1, full:], proj, weight)
            for g, piece in enumerate(pieces):
                done[g, slot] = piece

        @pl.loop(0, group)
        def _(member):
            step = turn * group + member

            @pl.when(step > 0)
            def _():
                back_copy(step).start()

            @pl.when(step == 0)
            def _():
                back_local.start()

    for kind in range(2):
        for step in range(1, cols):
            far_copy(step, kind).wait_send()
        for step in range(cols):
            for hop in range(1, subs):
                near_copy(step, hop, kind).wait_send()
    for step in range(1, strips):
        mod_copy(step).wait_send()
    back_local.wait()

    @pl.loop(1, total)
    def _(step):
        seq_copy(step).wait_send()
        back_copy(step).wait()


def travel(sequence, modulation, projection, out_weight, cols, subs):
    strips, per_owner, tokens, width = sequence.shape
    group = cols * subs
    slots = strips * per_owner // group
    total = strips * group
    sems = pltpu.SemaphoreType.DMA
    return pl.pallas_call(
        functools.partial(travel_kernel, strips, cols, subs),
        out_shape=jax.ShapeDtypeStruct((strips, per_owner, TILE, width), jnp.bfloat16),
        in_specs=[pl.BlockSpec(memory_space=pl.ANY)] * 4,
        out_specs=pl.BlockSpec(memory_space=pl.ANY),
        scratch_shapes=[
            pltpu.VMEM((group, slots, tokens, width), jnp.bfloat16),
            pltpu.VMEM((strips,) + modulation.shape, jnp.float32),
            pltpu.VMEM((group,) + projection.shape, jnp.bfloat16),
            pltpu.VMEM((group,) + out_weight.shape, jnp.bfloat16),
            pltpu.VMEM((group, slots, TILE, width), jnp.bfloat16),
            sems((total,)),
            sems((total,)),
            sems((total,)),
            sems((total,)),
            sems((strips,)),
            sems((strips,)),
            sems((2 * cols,)),
            sems((2 * cols,)),
            sems((2 * group,)),
            sems((2 * group,)),
            sems((5,)),
        ],
        compiler_params=pltpu.CompilerParams(
            collective_id=0, has_side_effects=True, vmem_limit_bytes=40 * 1024 * 1024
        ),
        name="travel",
    )(sequence, modulation, projection, out_weight)


def attend(inputs, scale, shift, projection, out_weight):
    parts, slots, tokens, width = inputs.shape
    full = parts * width
    whole = lambda s: (0, 0, 0, 0)
    return pl.pallas_call(
        attend_kernel,
        grid=(slots,),
        in_specs=[
            pl.BlockSpec((parts, 1, tokens, width), lambda s: (0, s, 0, 0)),
            pl.BlockSpec((1, 1, full), lambda s: (s, 0, 0)),
            pl.BlockSpec((1, 1, full), lambda s: (s, 0, 0)),
            pl.BlockSpec(projection.shape, whole),
            pl.BlockSpec(out_weight.shape, lambda s: (0, 0, 0)),
        ],
        out_specs=pl.BlockSpec((parts, 1, TILE, width), lambda s: (0, s, 0, 0)),
        out_shape=jax.ShapeDtypeStruct((parts, slots, TILE, width), jnp.bfloat16),
        compiler_params=pltpu.CompilerParams(vmem_limit_bytes=48 * 1024 * 1024),
        cost_estimate=pl.CostEstimate(
            flops=slots * 2 * tokens * full * full * 4,
            bytes_accessed=2 * (slots * 2 * tokens * full + 4 * full * full),
            transcendentals=slots * tokens * tokens * 8,
        ),
        name="attend",
    )(inputs, scale[:, None, :], shift[:, None, :], projection, out_weight)


def pick_rows(mod_table, first_slot, slot_total, per_source):
    sources = (first_slot + jnp.arange(slot_total, dtype=jnp.int32)) // per_source
    select = (sources[:, None] == jnp.arange(mod_table.shape[0], dtype=jnp.int32)[None, :]).astype(
        jnp.float32
    )
    return jnp.dot(select, mod_table, precision=lax.Precision.HIGHEST)


def body(
    fine_field,
    conv_taps,
    position_table,
    coarse_bands,
    band_weight,
    noise_step,
    land_tiles,
    tile_owner,
    neighbour_lists,
    tile_order,
    expert_projections,
    expert_output,
):
    lat_rows, lon_cells, channels = fine_field.shape
    tiles_row = land_tiles.shape[1]
    tile_count = lat_rows * tiles_row
    strips = lax.axis_size("row")
    per_owner = tile_count // strips
    padded = extended(fine_field, (("row", 0),), 1)
    padded = jnp.pad(padded, ((0, 0), (1, 1), (0, 0)))
    tap_values = conv_taps.astype(jnp.float32)
    running = fine_field.astype(jnp.float32)
    for row_shift in range(3):
        for col_shift in range(3):
            running = running + tap_values[row_shift, col_shift] * padded[
                row_shift : row_shift + lat_rows, col_shift : col_shift + lon_cells
            ].astype(jnp.float32)
    smoothed = running.astype(jnp.bfloat16)
    land_flat = land_tiles.reshape(tile_count)
    owner_flat = tile_owner.reshape(tile_count)
    tile_ids = jnp.arange(tile_count, dtype=jnp.int32)
    earlier = (
        (owner_flat[None, :] == owner_flat[:, None])
        & (land_flat[None, :] > 0)
        & (tile_ids[None, :] < tile_ids[:, None])
    )
    slot_rank = jnp.sum(earlier.astype(jnp.int32), axis=1)
    slot_of = owner_flat * per_owner + slot_rank
    chosen = ((slot_of[None, :] == tile_ids[:, None]) & (land_flat[None, :] > 0)).astype(jnp.int32)
    tile_of = jnp.sum(chosen * tile_ids[None, :], axis=1)
    starts = (tile_ids % tiles_row) * TILE
    index_table = jnp.concatenate(
        [
            tile_order.reshape(tile_count, TILE) + starts[:, None],
            neighbour_lists.reshape(tile_count, TILE),
        ],
        axis=1,
    ).T
    sequence = gather_tiles(smoothed, tile_of, index_table, position_table, tiles_row)
    outgoing = sequence.reshape(strips, per_owner, 2 * TILE, channels)
    group_size = lax.axis_size(("col", "sub"))
    my_slots = tile_count // group_size
    full_width = band_weight.shape[1] // 2
    own_proj = jnp.transpose(expert_projections[0], (1, 0, 2))
    if per_owner % group_size == 0:
        own_means = jnp.mean(coarse_bands.astype(jnp.float32), axis=2)
        own_mod = jnp.dot(
            own_means, band_weight.astype(jnp.float32), precision=lax.Precision.HIGHEST
        ) + step_embedding(noise_step, band_weight.shape[1])
        results = travel(
            outgoing,
            jnp.broadcast_to(own_mod, (8, band_weight.shape[1])),
            own_proj,
            expert_output[0],
            lax.axis_size("col"),
            lax.axis_size("sub"),
        )
    else:
        arrived = lax.all_to_all(outgoing, "row", split_axis=0, concat_axis=0, tiled=True)
        arrived = arrived.reshape(group_size, my_slots, 2 * TILE, channels)
        gathered_bands = lax.all_gather(coarse_bands, "row", axis=0, tiled=True)
        band_means = jnp.mean(gathered_bands.astype(jnp.float32), axis=2)
        modulation = jnp.dot(
            band_means, band_weight.astype(jnp.float32), precision=lax.Precision.HIGHEST
        ) + step_embedding(noise_step, band_weight.shape[1])
        inputs = lax.all_to_all(arrived, ("col", "sub"), split_axis=0, concat_axis=0, tiled=True)
        full_proj = lax.all_gather(
            own_proj, ("col", "sub"), axis=0, tiled=False
        )
        full_out = lax.all_gather(expert_output[0], ("col", "sub"), axis=0, tiled=False)
        local_mod = pick_rows(
            modulation, lax.axis_index(("col", "sub")) * my_slots, my_slots, per_owner
        )
        heads_out = attend(
            inputs, local_mod[:, :full_width], local_mod[:, full_width:], full_proj, full_out
        )
        returned = lax.all_to_all(heads_out, ("col", "sub"), split_axis=0, concat_axis=0, tiled=True)
        returned = returned.reshape(strips, per_owner, TILE, channels)
        results = lax.all_to_all(returned, "row", split_axis=0, concat_axis=0, tiled=True)
    results = results.reshape(tile_count, TILE, channels)
    return merge_tiles(
        smoothed, results, jnp.minimum(slot_of, tile_count - 1), land_flat, tile_order
    )


def solution(mesh):
    placed = (
        P(("grp", "row"), None, ("col", "sub")),
        P(None, None, ("col", "sub")),
        P(None, ("col", "sub")),
        P(("grp", "row"), None, None),
        P(),
        P(),
        P(("grp", "row"), None),
        P(("grp", "row"), None),
        P(("grp", "row"), None, None),
        P(("grp", "row"), None, None),
        P("row", None, None, ("col", "sub")),
        P("row", ("col", "sub"), None),
    )
    return jax.shard_map(
        body,
        mesh=mesh,
        in_specs=placed,
        out_specs=P(("grp", "row"), None, ("col", "sub")),
        check_vma=False,
    )
```
